32 devices in a mesh: trial: 2 (over y), ha: 4 (over z), wa: 4 (over x, core).
Axes of the slice: x: 2, y: 2, z: 4, core: 2. Of those that a mesh axis runs over, the one named last changes fastest.
Arguments:
- volume: bfloat16 [32, 256, 512], P(('trial', 'ha'), 'wa'), parts along dimension 0, may hold values from -6 to 6
- grad_out: bfloat16 [32, 256, 512], P(('trial', 'ha'), 'wa'), parts along dimension 0, may hold values from -12 to 12
- filter_one: float32 [27, 1024], replicated, may hold values from -4 to 4
- filter_two: float32 [27, 1024], replicated, may hold values from -4 to 4
- step_size: float32 [2], P('trial'), parts along dimension 0, may hold values from 0.05 to 0.5
Outputs:
- grad_input: bfloat16 [32, 256, 512], P(('trial', 'ha'), 'wa'), parts along dimension 0
- new_one: float32 [54, 1024], P('trial'), parts along dimension 0
- new_two: float32 [54, 1024], P('trial'), parts along dimension 0
The draws below stay inside these ranges and needn't reach their ends.
There are 2 independent parts, one for each index of `trial`. The reference program is written for one: setup_inputs(seed, part) draws one part's arguments, and reference() takes and returns one part's arrays. A program takes and returns all parts, laid end to end along the dimension named above; an argument that names none is the same for every part. Nothing has to cross between parts.
All inputs are finite; a program needn't handle non-finite values.
Results may differ from the reference program's by a relative error of at most 0.0024.
The reference program's roundings to bfloat16 on the way (of `act_one`, `grad_two` and `grad_one`) count: a program that leaves them out, or rounds other values in their place, can miss the bound.
Values may be sent and summed in bfloat16 or wider, within the bound.
A program may use at most 128 MiB of HBM per device.

```python
import math
import jax
import jax.numpy as jnp
from jax import lax

C = 32
DZ = 16
H = 16
W = 256


def draw_grad_out(key, part):
    shape = (H, W, DZ * C)
    values = jax.random.truncated_normal(key, -4.0, 4.0, shape, jnp.float32)
    heights = jnp.arange(H, dtype=jnp.float32) / max(H - 1, 1)
    factor = jnp.exp(heights * jnp.log(3.0))
    return (values * factor[:, None, None]).astype(jnp.bfloat16)


def level_of(key, shape, cuts, smallest, largest):
    level = 1.0
    for dim, parts in cuts:
        steps = jax.random.uniform(jax.random.fold_in(jax.random.fold_in(key, 6), dim), (parts,), jnp.float32, smallest / len(cuts), largest / len(cuts))
        level = level * jnp.repeat(jnp.exp(steps), shape[dim] // parts).reshape((-1,) + (1,) * (len(shape) - 1 - dim))
    return level


def noise(own_key, shape, spread, bound, cuts=(), kind=jnp.bfloat16):
    factor_of = level_of(own_key, shape, cuts, -0.22, 0.18) if cuts else 1.0
    array = jax.random.normal(own_key, shape, jnp.float32) * spread * factor_of
    return jnp.minimum(jnp.maximum(array, -bound), bound).astype(kind)


def setup_inputs(seed: int = 0, part: int = 0) -> dict:
    key_of = jax.random.split(jax.random.key(seed), 6)
    part_keys = jax.random.split(jax.random.fold_in(key_of[5], part), 6)
    volume = noise(part_keys[0], (H, W, DZ * C), 1.0, 6.0, ((0, 4), (1, 4)))
    grad_out = draw_grad_out(jax.random.fold_in(jax.random.fold_in(key_of[5], part), 71), part)
    filter_one = noise(key_of[2], (27, C * C), 1.0, 4.0, (), jnp.float32)
    filter_two = noise(key_of[3], (27, C * C), 1.0, 4.0, (), jnp.float32)
    step_size = jnp.clip(jnp.exp(jax.random.uniform(part_keys[4], (1,), jnp.float32, math.log(0.05), math.log(0.5))), 0.05, 0.5)
    return {"volume": volume, "grad_out": grad_out, "filter_one": filter_one, "filter_two": filter_two, "step_size": step_size}


SLOPE = 0.1

def smooth(values):
    return SLOPE * values + (1.0 - SLOPE) * (jax.nn.softplus(values) - math.log(2.0))

def slope_of(values):
    return SLOPE + (1.0 - SLOPE) * jax.nn.sigmoid(values)

def conv_same(field, kernel):
    rows, cols, merged = field.shape
    depth = merged // C
    shaped = field.astype(jnp.float32).reshape(1, rows, cols, depth, C)
    weights = kernel.astype(jnp.float32).reshape(3, 3, 3, C, C)
    result = lax.conv_general_dilated(shaped, weights, (1, 1, 1), ((1, 1), (1, 1), (1, 1)), dimension_numbers=('NDHWC', 'DHWIO', 'NDHWC'), precision=lax.Precision.HIGHEST)
    return result.reshape(rows, cols, merged)

def flipped(kernel):
    return kernel.reshape(3, 3, 3, C, C)[::-1, ::-1, ::-1].swapaxes(3, 4).reshape(27, C * C)

def filter_grad(field, grad):
    rows, cols, merged = grad.shape
    depth = merged // C
    padded = jnp.pad(field.astype(jnp.float32).reshape(rows, cols, depth, C), ((1, 1), (1, 1), (1, 1), (0, 0)))
    flat_grad = grad.astype(jnp.float32).reshape(-1, C)
    pieces = []
    for offset in range(27):
        row_off, col_off, dep_off = (offset // 9, offset // 3 % 3, offset % 3)
        window = padded[row_off:row_off + rows, col_off:col_off + cols, dep_off:dep_off + depth].reshape(-1, C)
        pieces.append(lax.dot_general(window, flat_grad, (((0,), (0,)), ((), ())), precision=lax.Precision.HIGHEST).reshape(-1))
    return jnp.stack(pieces)

def reference(volume, grad_out, filter_one, filter_two, step_size):
    scale = 1.0 / math.sqrt(27.0 * C)
    kernel_one = (filter_one * scale).astype(jnp.bfloat16)
    kernel_two = (filter_two * scale).astype(jnp.bfloat16)
    hidden_one = conv_same(volume, kernel_one)
    act_one = smooth(hidden_one).astype(jnp.bfloat16)
    hidden_two = conv_same(act_one, kernel_two)
    grad_two = (grad_out.astype(jnp.float32) * slope_of(hidden_two)).astype(jnp.bfloat16)
    grad_act = conv_same(grad_two, flipped(kernel_two))
    grad_one = (grad_act * slope_of(hidden_one)).astype(jnp.bfloat16)
    grad_input = conv_same(grad_one, flipped(kernel_one)).astype(jnp.bfloat16)
    sum_one = filter_grad(volume, grad_one)
    sum_two = filter_grad(act_one, grad_two)
    new_one = filter_one - step_size[0] * sum_one / jnp.sqrt(jnp.mean(sum_one * sum_one) + 1e-06)
    new_two = filter_two - step_size[0] * sum_two / jnp.sqrt(jnp.mean(sum_two * sum_two) + 1e-06)
    return (grad_input, new_one, new_two)
```

```python
import functools
import math

import jax
import jax.numpy as jnp
from jax import lax
from jax.experimental import pallas as pl
from jax.experimental.pallas import tpu as pltpu
from jax.sharding import PartitionSpec as P

C = 32
SLOPE = 0.1
LOG2 = math.log(2.0)
MESH = pl.DeviceIdType.MESH
SIDES = ((-1, 0), (1, 0), (0, -1), (0, 1), (-1, -1), (-1, 1), (1, -1), (1, 1))
OPPOSITE = (1, 0, 3, 2, 7, 6, 5, 4)


def kernel(
    high, wide, v_ref, g_ref, k_ref, out_ref, sums_ref,
    band, px, own, edge, row_in, edge_in, slope_one, gt, send_sem, recv_sem,
):
    rows, cols, lanes = v_ref.shape
    cells = rows * cols
    tiles = lanes // 128
    ih, iw = lax.axis_index("ha"), lax.axis_index("wa")
    f32, bf16 = jnp.float32, jnp.bfloat16

    def has(d):
        dh, dw = SIDES[d]
        ok = None
        for step, at, count in ((dh, ih, high), (dw, iw, wide)):
            if step:
                one = (at > 0) if step < 0 else (at < count - 1)
                ok = one if ok is None else jnp.logical_and(ok, one)
        return ok

    def target(d):
        return {"ha": ih + SIDES[d][0], "wa": iw + SIDES[d][1]}

    def landing(k, d):
        return row_in.at[k, d] if d < 2 else edge_in.at[k, d - 2]

    def copy_of(k, d):
        if d < 2:
            at = 0 if d == 0 else rows - 1
            source = v_ref.at[at] if k == 0 else own.at[k - 1, at]
        else:
            source = edge.at[k, 0 if SIDES[d][1] < 0 else 1]
        return pltpu.make_async_remote_copy(
            src_ref=source,
            dst_ref=landing(k, OPPOSITE[d]),
            send_sem=send_sem.at[k, d],
            recv_sem=recv_sem.at[k, OPPOSITE[d]],
            device_id=target(d),
            device_id_type=MESH,
        )

    def arrival_of(k, d):
        return pltpu.make_async_remote_copy(
            src_ref=landing(k, d),
            dst_ref=landing(k, d),
            send_sem=send_sem.at[k, d],
            recv_sem=recv_sem.at[k, d],
            device_id=target(d),
            device_id_type=MESH,
        )

    def set_edges(k, value):
        for r in range(rows):
            edge[k, 0, r : r + 1, :] = value[r, 0:1, :]
            edge[k, 1, r : r + 1, :] = value[r, cols - 1 : cols, :]

    def send(k):
        for d in range(8):
            @pl.when(has(d))
            def _():
                copy_of(k, d).start()

    def receive(k):
        for d in range(8):
            @pl.when(has(d))
            def _():
                arrival_of(k, d).wait_recv()

    def finish():
        for k in range(4):
            for d in range(8):
                @pl.when(has(d))
                def _():
                    copy_of(k, d).wait_send()

    col = lax.broadcasted_iota(jnp.int32, (cols, lanes), 0)

    def put_row(k, r, value, left, right):
        px[k, r, :, 0:lanes] = jnp.where(col == 0, left, pltpu.roll(value, 1, 0)).astype(bf16)
        px[k, r, :, lanes : 2 * lanes] = value.astype(bf16)
        px[k, r, :, 2 * lanes :] = jnp.where(
            col == cols - 1, right, pltpu.roll(value, cols - 1, 0)
        ).astype(bf16)

    def assemble(k, value):
        last = rows - 1
        for r in range(rows):
            put_row(k, r + 1, value[r], edge_in[k, 0, r : r + 1, :], edge_in[k, 1, r : r + 1, :])
        put_row(k, 0, row_in[k, 0].astype(f32),
                edge_in[k, 2, last : last + 1, :], edge_in[k, 3, last : last + 1, :])
        put_row(k, rows + 1, row_in[k, 1].astype(f32),
                edge_in[k, 4, 0:1, :], edge_in[k, 5, 0:1, :])

    def conv(k, f):
        total = jnp.zeros((cells, lanes), f32)
        for a in range(3):
            left = px[k, a : a + rows].reshape(cells, 3 * lanes)
            total += jnp.dot(left, band[f, a], preferred_element_type=f32)
        return total

    def conv_back(k, f):
        total = jnp.zeros((cells, lanes), f32)
        for a in range(3):
            for b in range(3):
                left = px[k, a : a + rows, :, b * lanes : (b + 1) * lanes].reshape(cells, lanes)
                right = band[f, 2 - a, (2 - b) * lanes : (3 - b) * lanes, :]
                total += lax.dot_general(
                    left, right, (((1,), (1,)), ((), ())), preferred_element_type=f32
                )
        return total

    def filter_sums(k, f, grad):
        gt[C : C + lanes, :] = grad.T.astype(bf16)
        group = lax.broadcasted_iota(jnp.int32, (C, 128), 1) // C
        for a in range(3):
            total = jnp.zeros((6 * C, 384), f32)
            for q in range(tiles):
                source = jnp.concatenate(
                    [
                        px[k, a : a + rows, :, b * lanes + q * 128 : b * lanes + (q + 1) * 128]
                        .reshape(cells, 128)
                        for b in range(3)
                    ],
                    axis=1,
                )
                total += jnp.dot(
                    gt[q * 128 : q * 128 + 6 * C, :], source, preferred_element_type=f32
                )
            for c in range(3):
                result = jnp.zeros((C, 128), f32)
                for b in range(3):
                    part = jnp.zeros((C, 128), f32)
                    for s in range(4):
                        at = (s + 2 - c) * C
                        block = total[at : at + C, b * 128 : (b + 1) * 128]
                        part = jnp.where(group == s, block, part)
                    part = part + pltpu.roll(part, 64, 1)
                    part = part + pltpu.roll(part, 32, 1)
                    result = jnp.where(group == b, part, result)
                sums_ref[f, a, c * C : (c + 1) * C, :] = result

    def build(f):
        lane = lax.broadcasted_iota(jnp.int32, (C, 128), 1)
        zero = jnp.zeros((C, 128), f32)
        for a in range(3):
            for b in range(3):
                strip = k_ref[f, a * 3 + b].astype(f32)
                turned = [
                    pltpu.roll(strip, 96, 1), strip, pltpu.roll(strip, 32, 1), pltpu.roll(strip, 64, 1)
                ]
                for s in range(4):
                    turn = turned[s]
                    low = high_part = zero
                    middle = turn
                    if s == 0:
                        middle = jnp.where(lane < 64, turn, 0.0)
                        low = jnp.where(lane >= 96, turn, 0.0)
                    if s == 3:
                        middle = jnp.where(lane >= 64, turn, 0.0)
                        high_part = jnp.where(lane < 32, turn, 0.0)
                    low, middle, high_part, none = (
                        x.astype(bf16) for x in (low, middle, high_part, zero)
                    )
                    for q in range(tiles):
                        at = b * lanes + q * 128 + s * C
                        for t in range(tiles):
                            block = {-1: low, 0: middle, 1: high_part}.get(t - q, none)
                            band[f, a, at : at + C, t * 128 : (t + 1) * 128] = block

    def sharing(values):
        small = jnp.exp(-jnp.abs(values))
        share = 1.0 / (1.0 + small)
        return small, SLOPE + (1.0 - SLOPE) * jnp.where(values >= 0, share, small * share)

    barrier = pltpu.get_barrier_semaphore()
    for d in range(8):
        @pl.when(has(d))
        def _():
            pl.semaphore_signal(barrier, inc=1, device_id=target(d), device_id_type=MESH)

    edge[...] = jnp.zeros(edge.shape, f32)
    gt[...] = jnp.zeros(gt.shape, bf16)
    for d in range(8):
        @pl.when(jnp.logical_not(has(d)))
        def _():
            for k in range(4):
                if d < 2:
                    row_in[k, d] = jnp.zeros((cols, lanes), bf16)
                else:
                    edge_in[k, d - 2] = jnp.zeros(edge.shape[2:], f32)
    volume = v_ref[...].astype(f32)
    set_edges(0, volume)
    tall = 1 + jnp.where(ih > 0, 1, 0) + jnp.where(ih < high - 1, 1, 0)
    broad = 1 + jnp.where(iw > 0, 1, 0) + jnp.where(iw < wide - 1, 1, 0)
    pl.semaphore_wait(barrier, tall * broad - 1)
    send(0)
    build(0)
    build(1)
    receive(0)
    assemble(0, v_ref[...].astype(f32))

    hidden = conv(0, 0)
    small, slope = sharing(hidden)
    slope_one[...] = slope
    soft = jnp.maximum(hidden, 0.0) + jnp.log(1.0 + small)
    act = (SLOPE * hidden + (1.0 - SLOPE) * (soft - LOG2)).astype(bf16).reshape(rows, cols, lanes)
    own[0] = act
    set_edges(1, act.astype(f32))
    send(1)
    receive(1)
    assemble(1, own[0].astype(f32))

    slope = sharing(conv(1, 1))[1]
    grad = (g_ref[...].astype(f32).reshape(cells, lanes) * slope).astype(bf16)
    own[1] = grad.reshape(rows, cols, lanes)
    set_edges(2, own[1].astype(f32))
    send(2)
    filter_sums(1, 1, own[1].astype(f32).reshape(cells, lanes))
    receive(2)
    assemble(2, own[1].astype(f32))

    grad = (conv_back(2, 1) * slope_one[...]).astype(bf16)
    own[2] = grad.reshape(rows, cols, lanes)
    set_edges(3, own[2].astype(f32))
    send(3)
    filter_sums(0, 0, own[2].astype(f32).reshape(cells, lanes))
    receive(3)
    assemble(3, own[2].astype(f32))

    out_ref[...] = conv_back(3, 0).astype(bf16).reshape(rows, cols, lanes)
    finish()


def strips(kernel_one):
    parts = kernel_one.reshape(9, 3, C, C)[:, ::-1].transpose(0, 2, 1, 3).reshape(9, C, 3 * C)
    return jnp.pad(parts, ((0, 0), (0, 0), (0, C)))


def per_device(volume, grad_out, filter_one, filter_two, step_size):
    scale = 1.0 / math.sqrt(27.0 * C)
    kernels = jnp.stack(
        [strips((f * scale).astype(jnp.bfloat16)) for f in (filter_one, filter_two)]
    )
    rows, cols, lanes = volume.shape
    tall = -(-rows // 8) * 8
    vmem = pl.BlockSpec(memory_space=pltpu.VMEM)
    grad_input, sums = pl.pallas_call(
        functools.partial(kernel, lax.axis_size("ha"), lax.axis_size("wa")),
        out_shape=(
            jax.ShapeDtypeStruct(volume.shape, jnp.bfloat16),
            jax.ShapeDtypeStruct((2, 3, 3 * C, 128), jnp.float32),
        ),
        in_specs=[vmem] * 3,
        out_specs=(vmem, vmem),
        scratch_shapes=[
            pltpu.VMEM((2, 3, 3 * lanes, lanes), jnp.bfloat16),
            pltpu.VMEM((4, rows + 2, cols, 3 * lanes), jnp.bfloat16),
            pltpu.VMEM((3, rows, cols, lanes), jnp.bfloat16),
            pltpu.VMEM((4, 2, tall, lanes), jnp.float32),
            pltpu.VMEM((4, 2, cols, lanes), jnp.bfloat16),
            pltpu.VMEM((4, 6, tall, lanes), jnp.float32),
            pltpu.VMEM((rows * cols, lanes), jnp.float32),
            pltpu.VMEM((lanes + 2 * C, rows * cols), jnp.bfloat16),
            pltpu.SemaphoreType.DMA((4, 8)),
            pltpu.SemaphoreType.DMA((4, 8)),
        ],
        compiler_params=pltpu.CompilerParams(
            collective_id=0, has_side_effects=True, vmem_limit_bytes=44 * 2**20
        ),
    )(volume, grad_out, kernels)
    totals = lax.psum(sums, ("ha", "wa"))
    totals = (
        totals.reshape(2, 3, 3, C, 4, C)[:, :, :, :, :3]
        .transpose(0, 1, 4, 2, 5, 3)
        .reshape(2, 27, C * C)
    )
    filters = jnp.stack([filter_one, filter_two])
    spread = jnp.sqrt(jnp.mean(totals * totals, axis=(1, 2)) + 1e-06)
    result = filters - step_size[0] * totals / spread[:, None, None]
    return (grad_input, result[0], result[1])


def solution(mesh):
    placed = (P(("trial", "ha"), "wa", None), P(("trial", "ha"), "wa", None), P(), P(), P("trial"))
    return jax.shard_map(
        per_device,
        mesh=mesh,
        in_specs=placed,
        out_specs=(P(("trial", "ha"), "wa", None), P("trial", None), P("trial", None)),
        check_vma=False,
    )
```

```python
import functools
import math

import jax
import jax.numpy as jnp
from jax import lax
from jax.experimental import pallas as pl
from jax.experimental.pallas import tpu as pltpu
from jax.sharding import PartitionSpec as P

C = 32
SLOPE = 0.1
LOG2 = math.log(2.0)
MESH = pl.DeviceIdType.MESH
SIDES = ((-1, 0), (1, 0), (0, -1), (0, 1), (-1, -1), (-1, 1), (1, -1), (1, 1))
OPPOSITE = (1, 0, 3, 2, 7, 6, 5, 4)


def kernel(
    high, wide, v_ref, g_ref, k_ref, f1_ref, f2_ref, step_ref, out_ref, new1_ref, new2_ref,
    band, px, own, edge, row_in, edge_in, slope_one, gt, part_ref, wa_in, ha_in, held, full, turned_ref,
    send_sem, recv_sem, wa_send, wa_recv, ha_send, ha_recv,
):
    rows, cols, lanes = v_ref.shape
    cells = rows * cols
    tiles = lanes // 128
    ih, iw = lax.axis_index("ha"), lax.axis_index("wa")
    f32, bf16 = jnp.float32, jnp.bfloat16

    def has(d):
        dh, dw = SIDES[d]
        ok = None
        for step, at, count in ((dh, ih, high), (dw, iw, wide)):
            if step:
                one = (at > 0) if step < 0 else (at < count - 1)
                ok = one if ok is None else jnp.logical_and(ok, one)
        return ok

    def target(d):
        return {"ha": ih + SIDES[d][0], "wa": iw + SIDES[d][1]}

    def landing(k, d):
        return row_in.at[k, d] if d < 2 else edge_in.at[k, d - 2]

    def copy_of(k, d):
        if d < 2:
            at = 0 if d == 0 else rows - 1
            source = v_ref.at[at] if k == 0 else own.at[k - 1, at]
        else:
            source = edge.at[k, 0 if SIDES[d][1] < 0 else 1]
        return pltpu.make_async_remote_copy(
            src_ref=source,
            dst_ref=landing(k, OPPOSITE[d]),
            send_sem=send_sem.at[k, d],
            recv_sem=recv_sem.at[k, OPPOSITE[d]],
            device_id=target(d),
            device_id_type=MESH,
        )

    def arrival_of(k, d):
        return pltpu.make_async_remote_copy(
            src_ref=landing(k, d),
            dst_ref=landing(k, d),
            send_sem=send_sem.at[k, d],
            recv_sem=recv_sem.at[k, d],
            device_id=target(d),
            device_id_type=MESH,
        )

    def set_edges(k, value):
        for r in range(rows):
            edge[k, 0, r : r + 1, :] = value[r, 0:1, :]
            edge[k, 1, r : r + 1, :] = value[r, cols - 1 : cols, :]

    def send(k):
        for d in range(8):
            @pl.when(has(d))
            def _():
                copy_of(k, d).start()

    def receive(k):
        for d in range(8):
            @pl.when(has(d))
            def _():
                arrival_of(k, d).wait_recv()

    def finish():
        for k in range(4):
            for d in range(8):
                @pl.when(has(d))
                def _():
                    copy_of(k, d).wait_send()
        for f in range(2):
            for stage in range(2):
                for j in range(1, wide):
                    wa_copy(f, stage, j).wait_send()
                for j in range(1, high):
                    ha_copy(f, stage, j).wait_send()

    col = lax.broadcasted_iota(jnp.int32, (cols, lanes), 0)

    def put_row(k, r, value, left, right):
        px[k, r, :, 0:lanes] = jnp.where(col == 0, left, pltpu.roll(value, 1, 0)).astype(bf16)
        px[k, r, :, lanes : 2 * lanes] = value.astype(bf16)
        px[k, r, :, 2 * lanes :] = jnp.where(
            col == cols - 1, right, pltpu.roll(value, cols - 1, 0)
        ).astype(bf16)

    def assemble(k, value):
        last = rows - 1
        for r in range(rows):
            put_row(k, r + 1, value[r], edge_in[k, 0, r : r + 1, :], edge_in[k, 1, r : r + 1, :])
        put_row(k, 0, row_in[k, 0].astype(f32),
                edge_in[k, 2, last : last + 1, :], edge_in[k, 3, last : last + 1, :])
        put_row(k, rows + 1, row_in[k, 1].astype(f32),
                edge_in[k, 4, 0:1, :], edge_in[k, 5, 0:1, :])

    def conv(k, f):
        total = jnp.zeros((cells, lanes), f32)
        for a in range(3):
            left = px[k, a : a + rows].reshape(cells, 3 * lanes)
            total += jnp.dot(left, band[f, a], preferred_element_type=f32)
        return total

    def conv_back(k, f):
        total = jnp.zeros((cells, lanes), f32)
        for a in range(3):
            for b in range(3):
                left = px[k, a : a + rows, :, b * lanes : (b + 1) * lanes].reshape(cells, lanes)
                right = band[f, 2 - a, (2 - b) * lanes : (3 - b) * lanes, :]
                total += lax.dot_general(
                    left, right, (((1,), (1,)), ((), ())), preferred_element_type=f32
                )
        return total

    def filter_sums(k, f, grad):
        gt[C : C + lanes, :] = grad.T.astype(bf16)
        group = lax.broadcasted_iota(jnp.int32, (C, 128), 1) // C
        for a in range(3):
            total = jnp.zeros((6 * C, 384), f32)
            for q in range(tiles):
                source = jnp.concatenate(
                    [
                        px[k, a : a + rows, :, b * lanes + q * 128 : b * lanes + (q + 1) * 128]
                        .reshape(cells, 128)
                        for b in range(3)
                    ],
                    axis=1,
                )
                total += jnp.dot(
                    gt[q * 128 : q * 128 + 6 * C, :], source, preferred_element_type=f32
                )
            for c in range(3):
                result = jnp.zeros((C, 128), f32)
                for b in range(3):
                    part = jnp.zeros((C, 128), f32)
                    for s in range(4):
                        at = (s + 2 - c) * C
                        block = total[at : at + C, b * 128 : (b + 1) * 128]
                        part = jnp.where(group == s, block, part)
                    part = part + pltpu.roll(part, 64, 1)
                    part = part + pltpu.roll(part, 32, 1)
                    result = jnp.where(group == b, part, result)
                at = (a * 3 + c) * C
                part_ref[f, at : at + C, :] = result

    piece = part_ref.shape[1] // (high * wide)
    stripe = high * piece

    def wa_copy(f, stage, j, arriving=False):
        peer = lax.rem(iw + (wide - j if arriving else j), wide)
        if stage == 0:
            source = part_ref.at[f, pl.ds(pl.multiple_of(peer * stripe, 8), stripe)]
            landed = wa_in.at[f, j - 1]
            if arriving:
                source = landed
        else:
            at = peer if arriving else iw
            source = landed = full.at[f, pl.ds(pl.multiple_of(at * stripe, 8), stripe)]
        return pltpu.make_async_remote_copy(
            src_ref=source, dst_ref=landed,
            send_sem=wa_send.at[f, stage, j - 1], recv_sem=wa_recv.at[f, stage, j - 1],
            device_id={"wa": peer}, device_id_type=MESH,
        )

    def ha_copy(f, stage, j, arriving=False):
        peer = lax.rem(ih + (high - j if arriving else j), high)
        if stage == 0:
            source = held.at[f, pl.ds(pl.multiple_of(peer * piece, 8), piece)]
            landed = ha_in.at[f, j - 1]
            if arriving:
                source = landed
        else:
            at = iw * stripe + (peer if arriving else ih) * piece
            source = landed = full.at[f, pl.ds(pl.multiple_of(at, 8), piece)]
        return pltpu.make_async_remote_copy(
            src_ref=source, dst_ref=landed,
            send_sem=ha_send.at[f, stage, j - 1], recv_sem=ha_recv.at[f, stage, j - 1],
            device_id={"ha": peer}, device_id_type=MESH,
        )

    def scatter_wa(f):
        for j in range(1, wide):
            wa_copy(f, 0, j).start()

    def scatter_ha(f):
        for j in range(1, wide):
            wa_copy(f, 0, j, True).wait_recv()
        total = part_ref[f, pl.ds(pl.multiple_of(iw * stripe, 8), stripe), :]
        for j in range(1, wide):
            total = total + wa_in[f, j - 1]
        held[f] = total
        for j in range(1, high):
            ha_copy(f, 0, j).start()

    def gather_ha(f):
        for j in range(1, high):
            ha_copy(f, 0, j, True).wait_recv()
        total = held[f, pl.ds(pl.multiple_of(ih * piece, 8), piece), :]
        for j in range(1, high):
            total = total + ha_in[f, j - 1]
        full[f, pl.ds(pl.multiple_of(iw * stripe + ih * piece, 8), piece), :] = total
        for j in range(1, high):
            ha_copy(f, 1, j).start()

    def gather_wa(f):
        for j in range(1, high):
            ha_copy(f, 1, j, True).wait_recv()
        for j in range(1, wide):
            wa_copy(f, 1, j).start()

    def update(f, filter_ref, new_ref):
        for j in range(1, wide):
            wa_copy(f, 1, j, True).wait_recv()
        total = full[f, 0 : 9 * C, :]
        mean = jnp.sum(total * total) / (27.0 * C * C)
        factor = step_ref[0] * lax.rsqrt(jnp.full((C, 128), mean + 1e-06, f32))
        for a in range(3):
            for c in range(3):
                at = (a * 3 + c) * C
                flat = (total[at : at + C, :] * factor).T
                for b in range(3):
                    to = (a * 9 + b * 3 + c) * C
                    turned_ref[f, to : to + C, 0:C] = flat[b * C : (b + 1) * C, :]
        group = lax.broadcasted_iota(jnp.int32, (27, 128), 1) // C
        for j in range(C // 4):
            wanted = jnp.zeros((27, 128), f32)
            for t in range(4):
                got = turned_ref[f, pl.ds(4 * j + t, 27, stride=C), :]
                wanted = jnp.where(group == t, pltpu.roll(got, t * C, 1) if t else got, wanted)
            new_ref[:, j * 128 : (j + 1) * 128] = filter_ref[:, j * 128 : (j + 1) * 128] - wanted

    def build(f):
        lane = lax.broadcasted_iota(jnp.int32, (C, 128), 1)
        zero = jnp.zeros((C, 128), f32)
        for a in range(3):
            for b in range(3):
                strip = k_ref[f, a * 3 + b].astype(f32)
                turned = [
                    pltpu.roll(strip, 96, 1), strip, pltpu.roll(strip, 32, 1), pltpu.roll(strip, 64, 1)
                ]
                for s in range(4):
                    turn = turned[s]
                    low = high_part = zero
                    middle = turn
                    if s == 0:
                        middle = jnp.where(lane < 64, turn, 0.0)
                        low = jnp.where(lane >= 96, turn, 0.0)
                    if s == 3:
                        middle = jnp.where(lane >= 64, turn, 0.0)
                        high_part = jnp.where(lane < 32, turn, 0.0)
                    low, middle, high_part, none = (
                        x.astype(bf16) for x in (low, middle, high_part, zero)
                    )
                    for q in range(tiles):
                        at = b * lanes + q * 128 + s * C
                        for t in range(tiles):
                            block = {-1: low, 0: middle, 1: high_part}.get(t - q, none)
                            band[f, a, at : at + C, t * 128 : (t + 1) * 128] = block

    def sharing(values):
        small = jnp.exp(-jnp.abs(values))
        share = 1.0 / (1.0 + small)
        return small, SLOPE + (1.0 - SLOPE) * jnp.where(values >= 0, share, small * share)

    barrier = pltpu.get_barrier_semaphore()
    for d in range(4, 8):
        @pl.when(has(d))
        def _():
            pl.semaphore_signal(barrier, inc=1, device_id=target(d), device_id_type=MESH)
    for j in range(1, wide):
        pl.semaphore_signal(
            barrier, inc=1, device_id={"wa": lax.rem(iw + j, wide)}, device_id_type=MESH
        )
    for j in range(1, high):
        pl.semaphore_signal(
            barrier, inc=1, device_id={"ha": lax.rem(ih + j, high)}, device_id_type=MESH
        )

    edge[...] = jnp.zeros(edge.shape, f32)
    gt[...] = jnp.zeros(gt.shape, bf16)
    turned_ref[...] = jnp.zeros(turned_ref.shape, f32)
    part_ref[:, 9 * C :, :] = jnp.zeros((2, part_ref.shape[1] - 9 * C, 128), f32)
    for d in range(8):
        @pl.when(jnp.logical_not(has(d)))
        def _():
            for k in range(4):
                if d < 2:
                    row_in[k, d] = jnp.zeros((cols, lanes), bf16)
                else:
                    edge_in[k, d - 2] = jnp.zeros(edge.shape[2:], f32)
    volume = v_ref[...].astype(f32)
    set_edges(0, volume)
    tall = jnp.where(ih > 0, 1, 0) + jnp.where(ih < high - 1, 1, 0)
    broad = jnp.where(iw > 0, 1, 0) + jnp.where(iw < wide - 1, 1, 0)
    pl.semaphore_wait(barrier, tall * broad + wide + high - 2)
    send(0)
    build(0)
    build(1)
    receive(0)
    assemble(0, v_ref[...].astype(f32))

    hidden = conv(0, 0)
    small, slope = sharing(hidden)
    slope_one[...] = slope
    soft = jnp.maximum(hidden, 0.0) + jnp.log(1.0 + small)
    act = (SLOPE * hidden + (1.0 - SLOPE) * (soft - LOG2)).astype(bf16).reshape(rows, cols, lanes)
    own[0] = act
    set_edges(1, act.astype(f32))
    send(1)
    receive(1)
    assemble(1, own[0].astype(f32))

    slope = sharing(conv(1, 1))[1]
    grad = (g_ref[...].astype(f32).reshape(cells, lanes) * slope).astype(bf16)
    own[1] = grad.reshape(rows, cols, lanes)
    set_edges(2, own[1].astype(f32))
    send(2)
    filter_sums(1, 1, own[1].astype(f32).reshape(cells, lanes))
    scatter_wa(1)
    receive(2)
    assemble(2, own[1].astype(f32))

    grad = (conv_back(2, 1) * slope_one[...]).astype(bf16)
    own[2] = grad.reshape(rows, cols, lanes)
    set_edges(3, own[2].astype(f32))
    send(3)
    scatter_ha(1)
    filter_sums(0, 0, own[2].astype(f32).reshape(cells, lanes))
    scatter_wa(0)
    gather_ha(1)
    receive(3)
    assemble(3, own[2].astype(f32))
    scatter_ha(0)
    gather_wa(1)
    out_ref[...] = conv_back(3, 0).astype(bf16).reshape(rows, cols, lanes)
    gather_ha(0)
    update(1, f2_ref, new2_ref)
    gather_wa(0)
    update(0, f1_ref, new1_ref)
    finish()


def strips(kernel_one):
    parts = kernel_one.reshape(9, 3, C, C)[:, ::-1].transpose(0, 2, 1, 3).reshape(9, C, 3 * C)
    return jnp.pad(parts, ((0, 0), (0, 0), (0, C)))


def per_device(volume, grad_out, filter_one, filter_two, step_size):
    scale = 1.0 / math.sqrt(27.0 * C)
    kernels = jnp.stack(
        [strips((f * scale).astype(jnp.bfloat16)) for f in (filter_one, filter_two)]
    )
    rows, cols, lanes = volume.shape
    tall = -(-rows // 8) * 8
    high, wide = lax.axis_size("ha"), lax.axis_size("wa")
    piece = -(-9 * C // (high * wide * 8)) * 8
    vmem = pl.BlockSpec(memory_space=pltpu.VMEM)
    return pl.pallas_call(
        functools.partial(kernel, high, wide),
        out_shape=(
            jax.ShapeDtypeStruct(volume.shape, jnp.bfloat16),
            jax.ShapeDtypeStruct(filter_one.shape, jnp.float32),
            jax.ShapeDtypeStruct(filter_two.shape, jnp.float32),
        ),
        in_specs=[vmem] * 5 + [pl.BlockSpec(memory_space=pltpu.SMEM)],
        out_specs=(vmem,) * 3,
        scratch_shapes=[
            pltpu.VMEM((2, 3, 3 * lanes, lanes), jnp.bfloat16),
            pltpu.VMEM((4, rows + 2, cols, 3 * lanes), jnp.bfloat16),
            pltpu.VMEM((3, rows, cols, lanes), jnp.bfloat16),
            pltpu.VMEM((4, 2, tall, lanes), jnp.float32),
            pltpu.VMEM((4, 2, cols, lanes), jnp.bfloat16),
            pltpu.VMEM((4, 6, tall, lanes), jnp.float32),
            pltpu.VMEM((rows * cols, lanes), jnp.float32),
            pltpu.VMEM((lanes + 2 * C, rows * cols), jnp.bfloat16),
            pltpu.VMEM((2, high * wide * piece, 128), jnp.float32),
            pltpu.VMEM((2, wide - 1, high * piece, 128), jnp.float32),
            pltpu.VMEM((2, high - 1, piece, 128), jnp.float32),
            pltpu.VMEM((2, high * piece, 128), jnp.float32),
            pltpu.VMEM((2, high * wide * piece, 128), jnp.float32),
            pltpu.VMEM((2, 27 * C, 128), jnp.float32),
            pltpu.SemaphoreType.DMA((4, 8)),
            pltpu.SemaphoreType.DMA((4, 8)),
            pltpu.SemaphoreType.DMA((2, 2, wide - 1)),
            pltpu.SemaphoreType.DMA((2, 2, wide - 1)),
            pltpu.SemaphoreType.DMA((2, 2, high - 1)),
            pltpu.SemaphoreType.DMA((2, 2, high - 1)),
        ],
        compiler_params=pltpu.CompilerParams(
            collective_id=0, has_side_effects=True, vmem_limit_bytes=44 * 2**20
        ),
    )(volume, grad_out, kernels, filter_one, filter_two, step_size)


def solution(mesh):
    placed = (P(("trial", "ha"), "wa", None), P(("trial", "ha"), "wa", None), P(), P(), P("trial"))
    return jax.shard_map(
        per_device,
        mesh=mesh,
        in_specs=placed,
        out_specs=(P(("trial", "ha"), "wa", None), P("trial", None), P("trial", None)),
        check_vma=False,
    )
```

```python
import functools
import math

import jax
import jax.numpy as jnp
from jax import lax
from jax.experimental import pallas as pl
from jax.experimental.pallas import tpu as pltpu
from jax.sharding import PartitionSpec as P

C = 32
SLOPE = 0.1
LOG2 = math.log(2.0)
MESH = pl.DeviceIdType.MESH
SIDES = ((-1, 0), (1, 0), (0, -1), (0, 1), (-1, -1), (-1, 1), (1, -1), (1, 1))
OPPOSITE = (1, 0, 3, 2, 7, 6, 5, 4)


def kernel(
    high, wide, v_any, g_any, f1_any, f2_any, step_ref, out_ref, new1_ref, new2_ref,
    band, px, own, edge, row_in, edge_in, slope_one, gt, part_ref, wa_in, ha_in, held, full, turned_ref,
    v_ref, g_ref, f1_ref, f2_ref,
    send_sem, recv_sem, wa_send, wa_recv, ha_send, ha_recv, load_sem,
):
    rows, cols, lanes = v_ref.shape
    cells = rows * cols
    tiles = lanes // 128
    ih, iw = lax.axis_index("ha"), lax.axis_index("wa")
    f32, bf16 = jnp.float32, jnp.bfloat16

    def has(d):
        dh, dw = SIDES[d]
        ok = None
        for step, at, count in ((dh, ih, high), (dw, iw, wide)):
            if step:
                one = (at > 0) if step < 0 else (at < count - 1)
                ok = one if ok is None else jnp.logical_and(ok, one)
        return ok

    def target(d):
        return {"ha": ih + SIDES[d][0], "wa": iw + SIDES[d][1]}

    def landing(k, d):
        return row_in.at[k, d] if d < 2 else edge_in.at[k, d - 2]

    def copy_of(k, d):
        if d < 2:
            at = 0 if d == 0 else rows - 1
            source = v_ref.at[at] if k == 0 else own.at[k - 1, at]
        else:
            source = edge.at[k, 0 if SIDES[d][1] < 0 else 1]
        return pltpu.make_async_remote_copy(
            src_ref=source,
            dst_ref=landing(k, OPPOSITE[d]),
            send_sem=send_sem.at[k, d],
            recv_sem=recv_sem.at[k, OPPOSITE[d]],
            device_id=target(d),
            device_id_type=MESH,
        )

    def arrival_of(k, d):
        return pltpu.make_async_remote_copy(
            src_ref=landing(k, d),
            dst_ref=landing(k, d),
            send_sem=send_sem.at[k, d],
            recv_sem=recv_sem.at[k, d],
            device_id=target(d),
            device_id_type=MESH,
        )

    def set_edges(k, value):
        for r in range(rows):
            edge[k, 0, r : r + 1, :] = value[r, 0:1, :]
            edge[k, 1, r : r + 1, :] = value[r, cols - 1 : cols, :]

    def send(k):
        for d in range(8):
            @pl.when(has(d))
            def _():
                copy_of(k, d).start()

    def receive(k):
        for d in range(8):
            @pl.when(has(d))
            def _():
                arrival_of(k, d).wait_recv()

    def finish():
        for k in range(4):
            for d in range(8):
                @pl.when(has(d))
                def _():
                    copy_of(k, d).wait_send()
        for f in range(2):
            for stage in range(2):
                for j in range(1, wide):
                    wa_copy(f, stage, j).wait_send()
                for j in range(1, high):
                    ha_copy(f, stage, j).wait_send()

    col = lax.broadcasted_iota(jnp.int32, (cols, lanes), 0)

    def put_row(k, r, value, left, right):
        px[k, r, :, 0:lanes] = jnp.where(col == 0, left, pltpu.roll(value, 1, 0)).astype(bf16)
        px[k, r, :, lanes : 2 * lanes] = value.astype(bf16)
        px[k, r, :, 2 * lanes :] = jnp.where(
            col == cols - 1, right, pltpu.roll(value, cols - 1, 0)
        ).astype(bf16)

    def assemble(k, value):
        last = rows - 1
        for r in range(rows):
            put_row(k, r + 1, value[r], edge_in[k, 0, r : r + 1, :], edge_in[k, 1, r : r + 1, :])
        put_row(k, 0, row_in[k, 0].astype(f32),
                edge_in[k, 2, last : last + 1, :], edge_in[k, 3, last : last + 1, :])
        put_row(k, rows + 1, row_in[k, 1].astype(f32),
                edge_in[k, 4, 0:1, :], edge_in[k, 5, 0:1, :])

    def conv(k, f, heights=(0, 1, 2)):
        total = jnp.zeros((cells, lanes), f32)
        for a in heights:
            left = px[k, a : a + rows].reshape(cells, 3 * lanes)
            total += jnp.dot(left, band[f, a], preferred_element_type=f32)
        return total

    def filter_sums(k, f, grad):
        gt[C : C + lanes, :] = grad.T.astype(bf16)
        group = lax.broadcasted_iota(jnp.int32, (C, 128), 1) // C
        for a in range(3):
            total = jnp.zeros((6 * C, 384), f32)
            for q in range(tiles):
                source = jnp.concatenate(
                    [
                        px[k, a : a + rows, :, b * lanes + q * 128 : b * lanes + (q + 1) * 128]
                        .reshape(cells, 128)
                        for b in range(3)
                    ],
                    axis=1,
                )
                total += jnp.dot(
                    gt[q * 128 : q * 128 + 6 * C, :], source, preferred_element_type=f32
                )
            for c in range(3):
                result = jnp.zeros((C, 128), f32)
                for b in range(3):
                    part = jnp.zeros((C, 128), f32)
                    for s in range(4):
                        at = (s + 2 - c) * C
                        block = total[at : at + C, b * 128 : (b + 1) * 128]
                        part = jnp.where(group == s, block, part)
                    part = part + pltpu.roll(part, 64, 1)
                    part = part + pltpu.roll(part, 32, 1)
                    result = jnp.where(group == b, part, result)
                at = (a * 3 + c) * C
                part_ref[f, at : at + C, :] = result

    piece = part_ref.shape[1] // (high * wide)
    stripe = high * piece

    def wa_copy(f, stage, j, arriving=False):
        peer = lax.rem(iw + (wide - j if arriving else j), wide)
        if stage == 0:
            source = part_ref.at[f, pl.ds(pl.multiple_of(peer * stripe, 8), stripe)]
            landed = wa_in.at[f, j - 1]
            if arriving:
                source = landed
        else:
            at = peer if arriving else iw
            source = landed = full.at[f, pl.ds(pl.multiple_of(at * stripe, 8), stripe)]
        return pltpu.make_async_remote_copy(
            src_ref=source, dst_ref=landed,
            send_sem=wa_send.at[f, stage, j - 1], recv_sem=wa_recv.at[f, stage, j - 1],
            device_id={"wa": peer}, device_id_type=MESH,
        )

    def ha_copy(f, stage, j, arriving=False):
        peer = lax.rem(ih + (high - j if arriving else j), high)
        if stage == 0:
            source = held.at[f, pl.ds(pl.multiple_of(peer * piece, 8), piece)]
            landed = ha_in.at[f, j - 1]
            if arriving:
                source = landed
        else:
            at = iw * stripe + (peer if arriving else ih) * piece
            source = landed = full.at[f, pl.ds(pl.multiple_of(at, 8), piece)]
        return pltpu.make_async_remote_copy(
            src_ref=source, dst_ref=landed,
            send_sem=ha_send.at[f, stage, j - 1], recv_sem=ha_recv.at[f, stage, j - 1],
            device_id={"ha": peer}, device_id_type=MESH,
        )

    def scatter_wa(f):
        for j in range(1, wide):
            wa_copy(f, 0, j).start()

    def scatter_ha(f):
        for j in range(1, wide):
            wa_copy(f, 0, j, True).wait_recv()
        total = part_ref[f, pl.ds(pl.multiple_of(iw * stripe, 8), stripe), :]
        for j in range(1, wide):
            total = total + wa_in[f, j - 1]
        held[f] = total
        for j in range(1, high):
            ha_copy(f, 0, j).start()

    def gather_ha(f):
        for j in range(1, high):
            ha_copy(f, 0, j, True).wait_recv()
        total = held[f, pl.ds(pl.multiple_of(ih * piece, 8), piece), :]
        for j in range(1, high):
            total = total + ha_in[f, j - 1]
        full[f, pl.ds(pl.multiple_of(iw * stripe + ih * piece, 8), piece), :] = total
        for j in range(1, high):
            ha_copy(f, 1, j).start()

    def gather_wa(f):
        for j in range(1, high):
            ha_copy(f, 1, j, True).wait_recv()
        for j in range(1, wide):
            wa_copy(f, 1, j).start()

    def update(f, filter_ref, new_ref):
        for j in range(1, wide):
            wa_copy(f, 1, j, True).wait_recv()
        total = full[f, 0 : 9 * C, :]
        mean = jnp.sum(total * total) / (27.0 * C * C)
        factor = step_ref[0] * lax.rsqrt(jnp.full((C, 128), mean + 1e-06, f32))
        for a in range(3):
            for c in range(3):
                at = (a * 3 + c) * C
                flat = (total[at : at + C, :] * factor).T
                for b in range(3):
                    to = (a * 9 + b * 3 + c) * C
                    turned_ref[f, to : to + C, 0:C] = flat[b * C : (b + 1) * C, :]
        group = lax.broadcasted_iota(jnp.int32, (27, 128), 1) // C
        for j in range(C // 4):
            wanted = jnp.zeros((27, 128), f32)
            for t in range(4):
                got = turned_ref[f, pl.ds(4 * j + t, 27, stride=C), :]
                wanted = jnp.where(group == t, pltpu.roll(got, t * C, 1) if t else got, wanted)
            new_ref[:, j * 128 : (j + 1) * 128] = filter_ref[:, j * 128 : (j + 1) * 128] - wanted

    def spread(f, filter_ref):
        scaled = (filter_ref[...] * (1.0 / math.sqrt(27.0 * C))).astype(bf16).astype(f32)
        for j in range(C // 4):
            tile = scaled[:, j * 128 : (j + 1) * 128]
            for t in range(4):
                turned_ref[f, pl.ds(4 * j + t, 27, stride=C), :] = (
                    pltpu.roll(tile, 128 - t * C, 1) if t else tile
                )

    def strip_of(f, a, b, back):
        group = lax.broadcasted_iota(jnp.int32, (C, 128), 1) // C
        blocks = []
        for c in range(3):
            at = (a * 9 + b * 3 + c) * C
            blocks.append(turned_ref[f, at : at + C, :])
        if back:
            blocks = [blocks[0], pltpu.roll(blocks[1], C, 1), pltpu.roll(blocks[2], 2 * C, 1)]
        else:
            blocks = [blocks[2], pltpu.roll(blocks[1], C, 1), pltpu.roll(blocks[0], 2 * C, 1)]
        strip = jnp.zeros((C, 128), f32)
        for c in range(3):
            strip = jnp.where(group == c, blocks[c], strip)
        if not back:
            return strip
        flat = jnp.concatenate([strip] * 4, axis=0).T
        strip = jnp.zeros((C, 128), f32)
        for c in range(3):
            strip = jnp.where(group == c, flat[c * C : (c + 1) * C, :], strip)
        return strip

    def build(f, back):
        m = f + 2 * back
        lane = lax.broadcasted_iota(jnp.int32, (C, 128), 1)
        zero = jnp.zeros((C, 128), f32)
        for a in range(3):
            for b in range(3):
                strip = strip_of(f, 2 - a if back else a, 2 - b if back else b, back)
                turned = [
                    pltpu.roll(strip, 96, 1), strip, pltpu.roll(strip, 32, 1), pltpu.roll(strip, 64, 1)
                ]
                for s in range(4):
                    turn = turned[s]
                    low = high_part = zero
                    middle = turn
                    if s == 0:
                        middle = jnp.where(lane < 64, turn, 0.0)
                        low = jnp.where(lane >= 96, turn, 0.0)
                    if s == 3:
                        middle = jnp.where(lane >= 64, turn, 0.0)
                        high_part = jnp.where(lane < 32, turn, 0.0)
                    low, middle, high_part, none = (
                        x.astype(bf16) for x in (low, middle, high_part, zero)
                    )
                    for q in range(tiles):
                        at = b * lanes + q * 128 + s * C
                        for t in range(tiles):
                            block = {-1: low, 0: middle, 1: high_part}.get(t - q, none)
                            band[m, a, at : at + C, t * 128 : (t + 1) * 128] = block

    def sharing(values):
        small = jnp.exp(-jnp.abs(values))
        share = 1.0 / (1.0 + small)
        return small, SLOPE + (1.0 - SLOPE) * jnp.where(values >= 0, share, small * share)

    loads = [
        pltpu.make_async_copy(source, landed, load_sem.at[n])
        for n, (source, landed) in enumerate(
            ((v_any, v_ref), (f1_any, f1_ref), (f2_any, f2_ref), (g_any, g_ref))
        )
    ]
    for load in loads:
        load.start()
    barrier = pltpu.get_barrier_semaphore()
    for d in range(4, 8):
        @pl.when(has(d))
        def _():
            pl.semaphore_signal(barrier, inc=1, device_id=target(d), device_id_type=MESH)
    for j in range(1, wide):
        pl.semaphore_signal(
            barrier, inc=1, device_id={"wa": lax.rem(iw + j, wide)}, device_id_type=MESH
        )
    for j in range(1, high):
        pl.semaphore_signal(
            barrier, inc=1, device_id={"ha": lax.rem(ih + j, high)}, device_id_type=MESH
        )

    edge[...] = jnp.zeros(edge.shape, f32)
    gt[...] = jnp.zeros(gt.shape, bf16)
    part_ref[:, 9 * C :, :] = jnp.zeros((2, part_ref.shape[1] - 9 * C, 128), f32)
    for d in range(8):
        @pl.when(jnp.logical_not(has(d)))
        def _():
            for k in range(4):
                if d < 2:
                    row_in[k, d] = jnp.zeros((cols, lanes), bf16)
                else:
                    edge_in[k, d - 2] = jnp.zeros(edge.shape[2:], f32)
    loads[0].wait()
    volume = v_ref[...].astype(f32)
    set_edges(0, volume)
    tall = jnp.where(ih > 0, 1, 0) + jnp.where(ih < high - 1, 1, 0)
    broad = jnp.where(iw > 0, 1, 0) + jnp.where(iw < wide - 1, 1, 0)
    pl.semaphore_wait(barrier, tall * broad + wide + high - 2)
    send(0)
    loads[1].wait()
    spread(0, f1_ref)
    build(0, 0)
    receive(0)
    assemble(0, v_ref[...].astype(f32))

    hidden = conv(0, 0)
    small, slope = sharing(hidden)
    slope_one[...] = slope
    soft = jnp.maximum(hidden, 0.0) + jnp.log(1.0 + small)
    act = (SLOPE * hidden + (1.0 - SLOPE) * (soft - LOG2)).astype(bf16).reshape(rows, cols, lanes)
    own[0] = act
    set_edges(1, act.astype(f32))
    send(1)
    loads[2].wait()
    spread(1, f2_ref)
    build(1, 0)
    receive(1)
    assemble(1, own[0].astype(f32))

    loads[3].wait()
    slope = sharing(conv(1, 1))[1]
    grad = (g_ref[...].astype(f32).reshape(cells, lanes) * slope).astype(bf16)
    own[1] = grad.reshape(rows, cols, lanes)
    set_edges(2, own[1].astype(f32))
    send(2)
    build(1, 1)
    filter_sums(1, 1, own[1].astype(f32).reshape(cells, lanes))
    scatter_wa(1)
    receive(2)
    assemble(2, own[1].astype(f32))

    grad = (conv(2, 3) * slope_one[...]).astype(bf16)
    own[2] = grad.reshape(rows, cols, lanes)
    set_edges(3, own[2].astype(f32))
    send(3)
    build(0, 1)
    scatter_ha(1)
    filter_sums(0, 0, own[2].astype(f32).reshape(cells, lanes))
    scatter_wa(0)
    gather_ha(1)
    receive(3)
    assemble(3, own[2].astype(f32))
    scatter_ha(0)
    gather_wa(1)
    early = conv(3, 2, (0, 1))
    gather_ha(0)
    out_ref[...] = (early + conv(3, 2, (2,))).astype(bf16).reshape(rows, cols, lanes)
    gather_wa(0)
    update(1, f2_ref, new2_ref)
    update(0, f1_ref, new1_ref)
    finish()


def per_device(volume, grad_out, filter_one, filter_two, step_size):
    rows, cols, lanes = volume.shape
    tall = -(-rows // 8) * 8
    high, wide = lax.axis_size("ha"), lax.axis_size("wa")
    piece = -(-9 * C // (high * wide * 8)) * 8
    vmem = pl.BlockSpec(memory_space=pltpu.VMEM)
    return pl.pallas_call(
        functools.partial(kernel, high, wide),
        out_shape=(
            jax.ShapeDtypeStruct(volume.shape, jnp.bfloat16),
            jax.ShapeDtypeStruct(filter_one.shape, jnp.float32),
            jax.ShapeDtypeStruct(filter_two.shape, jnp.float32),
        ),
        in_specs=[pl.BlockSpec(memory_space=pl.ANY)] * 4 + [pl.BlockSpec(memory_space=pltpu.SMEM)],
        out_specs=(vmem,) * 3,
        scratch_shapes=[
            pltpu.VMEM((4, 3, 3 * lanes, lanes), jnp.bfloat16),
            pltpu.VMEM((4, rows + 2, cols, 3 * lanes), jnp.bfloat16),
            pltpu.VMEM((3, rows, cols, lanes), jnp.bfloat16),
            pltpu.VMEM((4, 2, tall, lanes), jnp.float32),
            pltpu.VMEM((4, 2, cols, lanes), jnp.bfloat16),
            pltpu.VMEM((4, 6, tall, lanes), jnp.float32),
            pltpu.VMEM((rows * cols, lanes), jnp.float32),
            pltpu.VMEM((lanes + 2 * C, rows * cols), jnp.bfloat16),
            pltpu.VMEM((2, high * wide * piece, 128), jnp.float32),
            pltpu.VMEM((2, wide - 1, high * piece, 128), jnp.float32),
            pltpu.VMEM((2, high - 1, piece, 128), jnp.float32),
            pltpu.VMEM((2, high * piece, 128), jnp.float32),
            pltpu.VMEM((2, high * wide * piece, 128), jnp.float32),
            pltpu.VMEM((2, 27 * C, 128), jnp.float32),
            pltpu.VMEM(volume.shape, volume.dtype),
            pltpu.VMEM(grad_out.shape, grad_out.dtype),
            pltpu.VMEM(filter_one.shape, filter_one.dtype),
            pltpu.VMEM(filter_two.shape, filter_two.dtype),
            pltpu.SemaphoreType.DMA((4, 8)),
            pltpu.SemaphoreType.DMA((4, 8)),
            pltpu.SemaphoreType.DMA((2, 2, wide - 1)),
            pltpu.SemaphoreType.DMA((2, 2, wide - 1)),
            pltpu.SemaphoreType.DMA((2, 2, high - 1)),
            pltpu.SemaphoreType.DMA((2, 2, high - 1)),
            pltpu.SemaphoreType.DMA((4,)),
        ],
        compiler_params=pltpu.CompilerParams(
            collective_id=0, has_side_effects=True, vmem_limit_bytes=63 * 2**20
        ),
    )(volume, grad_out, filter_one, filter_two, step_size)


def solution(mesh):
    placed = (P(("trial", "ha"), "wa", None), P(("trial", "ha"), "wa", None), P(), P(), P("trial"))
    return jax.shard_map(
        per_device,
        mesh=mesh,
        in_specs=placed,
        out_specs=(P(("trial", "ha"), "wa", None), P("trial", None), P("trial", None)),
        check_vma=False,
    )
```
